32 devices in a mesh: groups: 2 (over x), chan: 16 (over z, y, core).
Axes of the slice: x: 2, y: 2, z: 4, core: 2. Of those that a mesh axis runs over, the one named last changes fastest.
Arguments:
- raw: float32 [128, 2, 4352], P(('groups', 'chan')), parts along dimension 0, may hold values from -6 to 6
- fir: float32 [255], replicated, may hold values from -0.375 to 0.375
- spatial_taps: float32 [9], replicated, may hold values from -2 to 2
- flags: int32 [128, 2], P(('groups', 'chan')), parts along dimension 0, may hold values 0 or 1
- keep: int32 [64], replicated, may hold values 0 or 1
Outputs:
- correlations: bfloat16 [128, 101, 64], P(('groups', 'chan')), parts along dimension 0
The draws below stay inside these ranges and needn't reach their ends.
There are 2 independent parts, one for each index of `groups`. The reference program is written for one: setup_inputs(seed, part) draws one part's arguments, and reference() takes and returns one part's arrays. A program takes and returns all parts, laid end to end along the dimension named above; an argument that names none is the same for every part. Nothing has to cross between parts.
All inputs are finite; a program needn't handle non-finite values. No bound on the sum of `flags` on one device may be relied on, other than what follows from the above.
Results may differ from the reference program's by a relative error of at most 0.0046.
Values may be sent and summed in bfloat16 or wider, within the bound.
A program may use at most 128 MiB of HBM per device.

```python
import math
import jax
import jax.numpy as jnp
from jax import lax

CH_DEV = 4
S = 2
W = 2
NT = 512
TAPS = 255
DEC = 4
SPAN = 9
LAGS = 101
CH = 64
NF = 256
TD = 1024
TRAW = 4352
HALF = 4
HALFLAG = 50
N_CHAN = 16


def place_ends(result, own_key, low, high):
    longest = result.shape.index(max(result.shape))
    spots = []
    for shift in (0, 1):
        where = [jax.random.randint(jax.random.fold_in(own_key, axis), (), 0, length) for axis, length in enumerate(result.shape)]
        where[longest] = (where[longest] + shift) % result.shape[longest]
        spots.append(tuple(where))
    return result.at[spots[0]].set(low).at[spots[1]].set(high)


def levels(rng, dims, split, least, largest):
    gain = 1.0
    for position, parts in split:
        draws = jax.random.uniform(jax.random.fold_in(jax.random.fold_in(rng, 6), position), (parts,), jnp.float32, least / len(split), largest / len(split))
        gain = gain * jnp.repeat(jnp.exp(draws), dims[position] // parts).reshape((-1,) + (1,) * (len(dims) - 1 - position))
    return gain


def scatter_about(key, dims, deviation, bound, shards=(), held_as=jnp.bfloat16):
    entries = jax.random.normal(key, dims, jnp.float32) * deviation
    if len(shards) > 0:
        entries = levels(key, dims, shards, -0.22, 0.18) * entries
    return jnp.clip(entries, min=-bound, max=bound).astype(held_as)


def setup_inputs(seed: int = 0, part: int = 0) -> dict:
    keys = jax.random.split(jax.random.key(seed), 6)
    part_keys = jax.random.split(jax.random.fold_in(keys[5], part), 6)
    return {
        "raw": scatter_about(part_keys[0], (CH, S, TRAW), 1.0, 6.0, ((0, 16),), jnp.float32),
        "fir": scatter_about(keys[1], (TAPS,), TAPS ** -0.5, 0.375, (), jnp.float32),
        "spatial_taps": scatter_about(keys[2], (SPAN,), SPAN ** -0.5, 2.0, (), jnp.float32),
        "flags": place_ends((jax.random.randint(part_keys[3], (CH, S), 0, 4) < 3).astype(jnp.int32), jax.random.fold_in(part_keys[3], 1), 0, 1),
        "keep": place_ends((jax.random.randint(keys[4], (CH,), 0, 4) < 3).astype(jnp.int32), jax.random.fold_in(keys[4], 1), 0, 1),
    }


def decimate(raw, fir):
    rows = raw.shape[0]
    segs = raw.shape[1]
    block = math.gcd(TD, 128)
    n_blocks = TD // block
    stride = DEC * block
    width = stride + TAPS + 1
    row_pos = jnp.arange(width, dtype=jnp.int32)[:, None] - DEC * jnp.arange(block, dtype=jnp.int32)[None, :]
    inside = (row_pos >= 0) & (row_pos < TAPS)
    toeplitz = jnp.where(inside, jnp.take(fir, jnp.clip(row_pos, 0, TAPS - 1)), 0.0).astype(jnp.float32)
    main_mat = toeplitz[:stride]
    tail_mat = toeplitz[stride:]
    extra = (n_blocks + 1) * stride - raw.shape[2]
    extended = jnp.concatenate([raw, jnp.zeros((rows, segs, extra), jnp.float32)], 2)
    blocks = extended.reshape(rows, segs, n_blocks + 1, stride)
    output = jnp.dot(blocks[:, :, :n_blocks], main_mat, precision=lax.Precision.HIGHEST, preferred_element_type=jnp.float32)
    output = output + jnp.dot(blocks[:, :, 1:, :TAPS + 1], tail_mat, precision=lax.Precision.HIGHEST, preferred_element_type=jnp.float32)
    return output.reshape(rows, segs, TD)

def spatial_filter(padded, spatial_taps, rows):
    filtered = spatial_taps[0] * padded[0:rows]
    for offset in range(1, SPAN):
        filtered = filtered + spatial_taps[offset] * padded[offset:offset + rows]
    return filtered

def tables():
    time_idx = jnp.arange(NT, dtype=jnp.int32)
    freq_idx = jnp.arange(NF, dtype=jnp.int32)
    phases = time_idx[:, None] * freq_idx[None, :] % NT
    angles = phases.astype(jnp.float32) * (2.0 * math.pi / NT)
    norm_factor = 1.0 / math.sqrt(NT)
    cosine = jnp.cos(angles) * norm_factor
    sine = -jnp.sin(angles) * norm_factor
    taper_win = 0.5 - 0.5 * jnp.cos(time_idx.astype(jnp.float32) * (2.0 * math.pi / NT))
    lag_idx = jnp.arange(LAGS, dtype=jnp.int32) - HALFLAG
    lag_phase = freq_idx[:, None] * lag_idx[None, :] % NT
    lag_angles = lag_phase.astype(jnp.float32) * (2.0 * math.pi / NT)
    one_sided = jnp.where(freq_idx == 0, 1.0, 2.0).astype(jnp.float32)[:, None] * (1.0 / (2.0 * math.sqrt(NF)))
    lag_table = jnp.concatenate([one_sided * jnp.cos(lag_angles), -one_sided * jnp.sin(lag_angles)], 0)
    return (cosine, sine, taper_win, lag_table)

def whiten(filtered, flags, cosine, sine, taper_win):
    rows = filtered.shape[0]
    tapered = filtered.reshape(rows, S, W, NT) * taper_win
    real_part = jnp.dot(tapered, cosine, precision=lax.Precision.HIGHEST, preferred_element_type=jnp.float32)
    imag_part = jnp.dot(tapered, sine, precision=lax.Precision.HIGHEST, preferred_element_type=jnp.float32)
    amplitude = jnp.sqrt(real_part * real_part + imag_part * imag_part)
    factor = flags.astype(jnp.float32)[:, :, None, None] / jnp.maximum(amplitude, 0.25)
    whitened = jnp.stack([(real_part * factor).astype(jnp.bfloat16), (imag_part * factor).astype(jnp.bfloat16)], 1)
    return whitened.reshape(rows, 2 * S * W, NF)

def reference(raw, fir, spatial_taps, flags, keep):
    cosine, sine, taper_win, lag_table = tables()
    decimated = decimate(raw, fir)
    padded = jnp.pad(decimated, ((HALF, HALF), (0, 0), (0, 0)))
    filtered = spatial_filter(padded, spatial_taps, CH)
    spectra = whiten(filtered, flags, cosine, sine, taper_win).astype(jnp.float32)
    half_rows = S * W
    rotated = jnp.concatenate([-spectra[:, half_rows:], spectra[:, :half_rows]], 1)
    flag_f = flags.astype(jnp.float32)
    chan_idx = jnp.arange(CH, dtype=jnp.int32)

    def one_block(first):
        mine = lax.dynamic_slice_in_dim(spectra, first, CH_DEV, 0)
        cross_re = jnp.einsum('iuf,juf->ijf', mine, spectra, precision=lax.Precision.HIGHEST)
        cross_im = jnp.einsum('iuf,juf->ijf', mine, rotated, precision=lax.Precision.HIGHEST)
        summed = jnp.einsum('ijg,gl->ilj', jnp.concatenate([cross_re, cross_im], 2), lag_table, precision=lax.Precision.HIGHEST)
        counts = jnp.dot(lax.dynamic_slice_in_dim(flag_f, first, CH_DEV, 0), flag_f.T, precision=lax.Precision.HIGHEST)
        row_ids = first + jnp.arange(CH_DEV, dtype=jnp.int32)
        distance = jnp.abs(row_ids[:, None] - chan_idx[None, :])
        row_mask = (jnp.take(keep, distance) * (distance > 0)).astype(jnp.float32)
        factor = row_mask / jnp.maximum(counts, 1.0)
        return (summed * factor[:, None, :]).astype(jnp.bfloat16)
    firsts = jnp.arange(N_CHAN, dtype=jnp.int32) * CH_DEV
    blocks = lax.map(one_block, firsts)
    return blocks.reshape(CH, LAGS, CH)
```

```python
import functools
import math

import jax
import jax.numpy as jnp
import ml_dtypes
import numpy as np
from jax import lax
from jax.experimental import pallas as pl
from jax.experimental.pallas import tpu as pltpu
from jax.sharding import PartitionSpec as P

S = 2
W = 2
NT = 512
TAPS = 255
DEC = 4
SPAN = 9
LAGS = 101
NF = 256
TD = 1024
HALFLAG = 50
ROWS = 32
LAG_ROWS = 112
BLOCK = 128
REACH = DEC * BLOCK + TAPS + 1
COLS = 16
MESH = pl.DeviceIdType.MESH


def halves(values):
    high = values.astype(ml_dtypes.bfloat16)
    return high, (values - high.astype(np.float64)).astype(ml_dtypes.bfloat16)


def dft_table():
    time = np.arange(NT)
    angles = (time[:, None] * np.arange(NF)[None, :] % NT) * (2.0 * math.pi / NT)
    taper = (0.5 - 0.5 * np.cos(time * (2.0 * math.pi / NT))) / math.sqrt(NT)
    sine = -np.sin(angles)
    sine[:, 0] = 0.0
    table = np.concatenate([np.cos(angles), sine], 1) * taper[:, None]
    return np.concatenate(halves(table), 1)


def lag_table():
    freq = np.arange(NF)
    lags = np.arange(LAGS) - HALFLAG
    angles = (lags[:, None] * freq[None, :] % NT) * (2.0 * math.pi / NT)
    one_sided = np.where(freq == 0, 1.0, 2.0) / (2.0 * math.sqrt(NF))
    table = np.zeros((LAG_ROWS, 2 * NF))
    table[:LAGS, :NF] = one_sided * np.cos(angles)
    table[:LAGS, NF:] = -one_sided * np.sin(angles)
    table[:LAGS, NF] = 0.0
    table[LAGS, NF] = 0.5
    return np.concatenate(halves(table), 0)


def split(values):
    high = values.astype(jnp.bfloat16)
    return high, (values - high.astype(jnp.float32)).astype(jnp.bfloat16)


def product_nt(left, right):
    return lax.dot_general(
        left, right, (((1,), (1,)), ((), ())), preferred_element_type=jnp.float32
    )


def kernel(
    n,
    raw_ref,
    fir_ref,
    taps_ref,
    flags_ref,
    keep_ref,
    dft_hbm,
    lag_hbm,
    out_ref,
    dft_ref,
    lag_ref,
    firs_ref,
    pad_ref,
    filt_ref,
    dup_ref,
    spec_ref,
    turn_ref,
    own_ref,
    own_turn_ref,
    all_ref,
    cross_hi_ref,
    cross_lo_ref,
    table_sem,
    halo_send,
    halo_recv,
    send_sem,
    recv_sem,
):
    me = lax.axis_index("chan")
    total_ch = 4 * n

    dft_copy = pltpu.make_async_copy(dft_hbm, dft_ref, table_sem.at[0])
    lag_copy = pltpu.make_async_copy(lag_hbm, lag_ref, table_sem.at[1])
    dft_copy.start()
    lag_copy.start()

    barrier = pltpu.get_barrier_semaphore()

    def greet(k, carry):
        peer = lax.rem(me + k, n)
        pl.semaphore_signal(barrier, inc=1, device_id={"chan": peer}, device_id_type=MESH)
        return carry

    lax.fori_loop(1, n, greet, 0)

    firs_ref[...] = jnp.zeros_like(firs_ref)
    firs_ref[:, 0:TAPS] = jnp.broadcast_to(fir_ref[...], (32, TAPS))
    shifted = firs_ref[...]
    row_id = lax.broadcasted_iota(jnp.int32, shifted.shape, 0)
    for bit in range(5):
        moved = pltpu.roll(shifted, DEC << bit, 1)
        shifted = jnp.where((row_id // (1 << bit)) % 2 == 1, moved, shifted)
    pieces = []
    for part in range(4):
        row = []
        if part:
            row.append(jnp.zeros((32, 128 * part), jnp.float32))
        row.append(shifted)
        if part < 3:
            row.append(jnp.zeros((32, REACH - 384 - 128 * part), jnp.float32))
        pieces.append(jnp.concatenate(row, 1))
    filter_hi, filter_lo = split(jnp.concatenate(pieces, 0))
    raw = jnp.concatenate([raw_ref[c] for c in range(4)], 0)
    blocks = jnp.concatenate(
        [raw[:, DEC * BLOCK * b : DEC * BLOCK * b + REACH] for b in range(TD // BLOCK)], 0
    )
    raw_hi, raw_lo = split(blocks)
    sums = product_nt(
        jnp.concatenate([raw_hi, raw_lo], 0), jnp.concatenate([filter_hi, filter_lo], 0)
    )
    count = 8 * (TD // BLOCK)
    sums = sums[:count, :BLOCK] + (
        sums[count:, :BLOCK] + sums[:count, BLOCK:] + sums[count:, BLOCK:]
    )
    for b in range(TD // BLOCK):
        pad_ref[8:16, BLOCK * b : BLOCK * (b + 1)] = sums[8 * b : 8 * b + 8]

    pl.semaphore_wait(barrier, n - 1)

    to_right = pltpu.make_async_remote_copy(
        src_ref=pad_ref.at[8:16],
        dst_ref=pad_ref.at[0:8],
        send_sem=halo_send.at[0],
        recv_sem=halo_recv.at[0],
        device_id={"chan": lax.rem(me + 1, n)},
        device_id_type=MESH,
    )
    to_left = pltpu.make_async_remote_copy(
        src_ref=pad_ref.at[8:16],
        dst_ref=pad_ref.at[16:24],
        send_sem=halo_send.at[1],
        recv_sem=halo_recv.at[1],
        device_id={"chan": lax.rem(me + n - 1, n)},
        device_id_type=MESH,
    )

    @pl.when(me < n - 1)
    def _():
        to_right.start()

    @pl.when(me > 0)
    def _():
        to_left.start()

    masks = []
    keep = jnp.broadcast_to(keep_ref[...].astype(jnp.float32), (16, total_ch))
    keep = keep.astype(jnp.bfloat16)
    for chunk in range(n // COLS):
        lane = lax.broadcasted_iota(jnp.int32, (total_ch, 4 * 4 * COLS), 1)
        dist = lax.broadcasted_iota(jnp.int32, (total_ch, 4 * 4 * COLS), 0)
        gap = jnp.abs(
            4 * me + lane // (4 * COLS) - (lane % (4 * COLS) + chunk * 4 * COLS)
        )
        hit = jnp.where((gap == dist) & (dist > 0), 1.0, 0.0).astype(jnp.bfloat16)
        masks.append(jnp.dot(keep, hit, preferred_element_type=jnp.float32)[0:1])

    @pl.when(me > 0)
    def _():
        to_right.wait_recv()

    @pl.when(me == 0)
    def _():
        pad_ref[0:8] = jnp.zeros((8, TD), jnp.float32)

    @pl.when(me < n - 1)
    def _():
        to_left.wait_recv()

    @pl.when(me == n - 1)
    def _():
        pad_ref[16:24] = jnp.zeros((8, TD), jnp.float32)

    filtered = taps_ref[0] * pad_ref[0:8]
    for offset in range(1, SPAN):
        filtered = filtered + taps_ref[offset] * pad_ref[2 * offset : 2 * offset + 8]
    for tile in range(TD // 128):
        filt_ref[8 * tile : 8 * tile + 8] = filtered[:, 128 * tile : 128 * (tile + 1)]
    for s in range(S):
        for tile in range(TD // 128):
            one = filt_ref[pl.ds(8 * tile + s, 4, stride=2), :]
            dup_ref[8 * s : 8 * s + 4, 128 * tile : 128 * (tile + 1)] = one
            dup_ref[8 * s + 4 : 8 * s + 8, 128 * tile : 128 * (tile + 1)] = one
    windows = jnp.concatenate(
        [dup_ref[8 * s : 8 * s + 8, NT * w : NT * (w + 1)] for s in range(S) for w in range(W)], 0
    )
    win_hi, win_lo = split(windows)
    dft_copy.wait()
    spectra = jnp.dot(
        jnp.concatenate([win_hi, win_lo], 0), dft_ref[...], preferred_element_type=jnp.float32
    )
    spectra = spectra[:ROWS, : 2 * NF] + (
        spectra[ROWS:, : 2 * NF] + spectra[:ROWS, 2 * NF :] + spectra[ROWS:, 2 * NF :]
    )
    real, imag = spectra[:, :NF], spectra[:, NF:]
    rows = lax.broadcasted_iota(jnp.int32, (ROWS, NF), 0)
    lanes = lax.broadcasted_iota(jnp.int32, (ROWS, NF), 1)
    flag = jnp.zeros((ROWS, NF), jnp.float32)
    for s in range(S):
        for c in range(4):
            here = (rows // 16 == s) & (rows % 4 == c)
            flag = jnp.where(here, flags_ref[c, s].astype(jnp.float32), flag)
    factor = flag / jnp.maximum(jnp.sqrt(real * real + imag * imag), 0.25)
    is_real = (rows // 4) % 2 == 0
    real = (real * factor).astype(jnp.bfloat16).astype(jnp.float32)
    imag = (imag * factor).astype(jnp.bfloat16).astype(jnp.float32)
    stash = (lanes == 0) & (~is_real)
    spec = jnp.where(is_real, real, imag)
    all_ref[me] = jnp.where(stash, flag, spec).astype(jnp.bfloat16)

    def copy_to(k):
        return pltpu.make_async_remote_copy(
            src_ref=all_ref.at[me],
            dst_ref=all_ref.at[me],
            send_sem=send_sem.at[k],
            recv_sem=recv_sem.at[me],
            device_id={"chan": lax.rem(me + k, n)},
            device_id_type=MESH,
        )

    def send(k, carry):
        copy_to(k).start()
        return carry

    lax.fori_loop(1, n, send, 0)

    spec_ref[...] = jnp.where(stash, 0.0, spec)
    turn_ref[...] = jnp.where(stash, flag, jnp.where(is_real, imag, -real))
    upper = lax.broadcasted_iota(jnp.int32, (8, NF), 0) < 4
    for ref, target in ((spec_ref, own_ref), (turn_ref, own_turn_ref)):
        for i in range(4):
            for k in range(S * W):
                first = jnp.broadcast_to(ref[8 * k + i : 8 * k + i + 1], (8, NF))
                second = jnp.broadcast_to(ref[8 * k + 4 + i : 8 * k + 5 + i], (8, NF))
                target[i, 8 * k : 8 * k + 8] = jnp.where(upper, first, second)
    lag_copy.wait()

    def receive(k, carry):
        src = lax.rem(me + k, n)
        pltpu.make_async_remote_copy(
            src_ref=all_ref.at[src],
            dst_ref=all_ref.at[src],
            send_sem=send_sem.at[k],
            recv_sem=recv_sem.at[src],
            device_id={"chan": src},
            device_id_type=MESH,
        ).wait_recv()
        return carry

    lax.fori_loop(1, n, receive, 0)

    for chunk in range(n // COLS):

        def quad(q, carry):
            base = chunk * COLS + 4 * q
            for i in range(4):
                for half, ref in enumerate((own_ref, own_turn_ref)):
                    sums = []
                    for d in range(4):
                        theirs = all_ref[base + d].astype(jnp.float32)
                        acc = ref[i, 0:8] * theirs[0:8]
                        for k in range(1, S * W):
                            acc = acc + ref[i, 8 * k : 8 * k + 8] * theirs[8 * k : 8 * k + 8]
                        sums.append(acc)
                    both = []
                    for d in (0, 2):
                        a, b = sums[d], sums[d + 1]
                        both.append(
                            jnp.where(upper, a, b) + pltpu.roll(jnp.where(upper, b, a), 4, 0)
                        )
                    high, low = split(jnp.concatenate(both, 0))
                    at = pl.ds(pl.multiple_of(4 * COLS * i + 16 * q, 16), 16)
                    cross_hi_ref[at, NF * half : NF * (half + 1)] = high
                    cross_lo_ref[at, NF * half : NF * (half + 1)] = low
            return carry

        lax.fori_loop(0, COLS // 4, quad, 0)
        lag = lag_ref[...]
        summed = product_nt(lag, cross_hi_ref[...])
        summed = (
            summed[:LAG_ROWS]
            + summed[LAG_ROWS:]
            + product_nt(lag[:LAG_ROWS], cross_lo_ref[...])
        )
        scale = masks[chunk] / jnp.maximum(summed[LAGS : LAGS + 1], 1.0)
        result = (summed * scale).astype(jnp.bfloat16)
        for i in range(4):
            out_ref[i, :, 4 * COLS * chunk : 4 * COLS * (chunk + 1)] = result[
                :LAGS, 4 * COLS * i : 4 * COLS * (i + 1)
            ]

    def sent(k, carry):
        copy_to(k).wait_send()
        return carry

    lax.fori_loop(1, n, sent, 0)

    @pl.when(me < n - 1)
    def _():
        to_right.wait_send()

    @pl.when(me > 0)
    def _():
        to_left.wait_send()


def on_device(raw, fir, spatial_taps, flags, keep):
    n = lax.axis_size("chan")
    vmem = pl.BlockSpec(memory_space=pltpu.VMEM)
    smem = pl.BlockSpec(memory_space=pltpu.SMEM)
    anywhere = pl.BlockSpec(memory_space=pl.ANY)
    return pl.pallas_call(
        functools.partial(kernel, n),
        out_shape=jax.ShapeDtypeStruct((4, LAGS, 4 * n), jnp.bfloat16),
        in_specs=[vmem, vmem, smem, smem, vmem, anywhere, anywhere],
        out_specs=vmem,
        scratch_shapes=[
            pltpu.VMEM((NT, 4 * NF), jnp.bfloat16),
            pltpu.VMEM((2 * LAG_ROWS, 2 * NF), jnp.bfloat16),
            pltpu.VMEM((32, 384), jnp.float32),
            pltpu.VMEM((24, TD), jnp.float32),
            pltpu.VMEM((TD // 16, 128), jnp.float32),
            pltpu.VMEM((16, TD), jnp.float32),
            pltpu.VMEM((ROWS, NF), jnp.float32),
            pltpu.VMEM((ROWS, NF), jnp.float32),
            pltpu.VMEM((4, ROWS, NF), jnp.float32),
            pltpu.VMEM((4, ROWS, NF), jnp.float32),
            pltpu.VMEM((n, ROWS, NF), jnp.bfloat16),
            pltpu.VMEM((16 * COLS, 2 * NF), jnp.bfloat16),
            pltpu.VMEM((16 * COLS, 2 * NF), jnp.bfloat16),
            pltpu.SemaphoreType.DMA((2,)),
            pltpu.SemaphoreType.DMA((2,)),
            pltpu.SemaphoreType.DMA((2,)),
            pltpu.SemaphoreType.DMA((n,)),
            pltpu.SemaphoreType.DMA((n,)),
        ],
        compiler_params=pltpu.CompilerParams(
            collective_id=0, has_side_effects=True, vmem_limit_bytes=32 * 2**20
        ),
    )(
        raw,
        fir.reshape(1, TAPS),
        spatial_taps,
        flags,
        keep.reshape(1, 4 * n),
        jnp.asarray(dft_table()),
        jnp.asarray(lag_table()),
    )


def solution(mesh):
    placed = (P(("groups", "chan"), None, None), P(), P(), P(("groups", "chan"), None), P())
    return jax.shard_map(
        on_device,
        mesh=mesh,
        in_specs=placed,
        out_specs=P(("groups", "chan"), None, None),
        check_vma=False,
    )
```

```python
import functools
import math

import jax
import jax.numpy as jnp
import ml_dtypes
import numpy as np
from jax import lax
from jax.experimental import pallas as pl
from jax.experimental.pallas import tpu as pltpu
from jax.sharding import PartitionSpec as P

S = 2
W = 2
NT = 512
TAPS = 255
DEC = 4
SPAN = 9
LAGS = 101
NF = 256
TD = 1024
HALFLAG = 50
ROWS = 32
LAG_ROWS = 128
BLOCK = 128
REACH = DEC * BLOCK + TAPS + 1
COLS = 16
MESH = pl.DeviceIdType.MESH


def halves(values):
    high = values.astype(ml_dtypes.bfloat16)
    return high, (values - high.astype(np.float64)).astype(ml_dtypes.bfloat16)


def dft_table():
    time = np.arange(NT)
    angles = (time[:, None] * np.arange(NF)[None, :] % NT) * (2.0 * math.pi / NT)
    taper = (0.5 - 0.5 * np.cos(time * (2.0 * math.pi / NT))) / math.sqrt(NT)
    sine = -np.sin(angles)
    sine[:, 0] = 0.0
    table = np.concatenate([np.cos(angles), sine], 1) * taper[:, None]
    return np.concatenate(halves(table), 1)


def lag_table():
    freq = np.arange(NF)
    lags = np.arange(LAGS) - HALFLAG
    angles = (lags[:, None] * freq[None, :] % NT) * (2.0 * math.pi / NT)
    one_sided = np.where(freq == 0, 1.0, 2.0) / (2.0 * math.sqrt(NF))
    table = np.zeros((LAG_ROWS, 2 * NF))
    table[:LAGS, :NF] = one_sided * np.cos(angles)
    table[:LAGS, NF:] = -one_sided * np.sin(angles)
    table[:LAGS, NF] = 0.0
    table[LAGS, NF] = 0.5
    return np.concatenate(halves(table), 0)


def split(values):
    high = values.astype(jnp.bfloat16)
    return high, (values - high.astype(jnp.float32)).astype(jnp.bfloat16)


def product_nt(left, right):
    return lax.dot_general(
        left, right, (((1,), (1,)), ((), ())), preferred_element_type=jnp.float32
    )


def kernel(
    n,
    raw_hbm,
    fir_hbm,
    taps_hbm,
    flags_hbm,
    keep_hbm,
    dft_hbm,
    lag_hbm,
    out_ref,
    raw_ref,
    fir_ref,
    taps_ref,
    flags_ref,
    keep_ref,
    dft_ref,
    lag_ref,
    firs_ref,
    pad_ref,
    filt_ref,
    dup_ref,
    spec_ref,
    turn_ref,
    own_ref,
    own_turn_ref,
    all_ref,
    cross_hi_ref,
    cross_lo_ref,
    table_sem,
    halo_send,
    halo_recv,
    send_sem,
    recv_sem,
):
    me = lax.axis_index("chan")
    total_ch = 4 * n

    pairs = (
        (fir_hbm, fir_ref),
        (raw_hbm, raw_ref),
        (dft_hbm, dft_ref),
        (taps_hbm, taps_ref),
        (flags_hbm, flags_ref),
        (keep_hbm, keep_ref),
        (lag_hbm, lag_ref),
    )
    copies = [
        pltpu.make_async_copy(src, dst, table_sem.at[k]) for k, (src, dst) in enumerate(pairs)
    ]
    for copy in copies:
        copy.start()
    fir_copy, raw_copy, dft_copy, taps_copy, flags_copy, keep_copy, lag_copy = copies

    barrier = pltpu.get_barrier_semaphore()

    def greet(k, carry):
        peer = lax.rem(me + k, n)
        pl.semaphore_signal(barrier, inc=1, device_id={"chan": peer}, device_id_type=MESH)
        return carry

    lax.fori_loop(1, n, greet, 0)

    firs_ref[...] = jnp.zeros_like(firs_ref)
    fir_copy.wait()
    firs_ref[:, 0:TAPS] = jnp.broadcast_to(fir_ref[...], (32, TAPS))
    shifted = firs_ref[...]
    row_id = lax.broadcasted_iota(jnp.int32, shifted.shape, 0)
    for bit in range(5):
        moved = pltpu.roll(shifted, DEC << bit, 1)
        shifted = jnp.where((row_id // (1 << bit)) % 2 == 1, moved, shifted)
    pieces = []
    for part in range(4):
        row = []
        if part:
            row.append(jnp.zeros((32, 128 * part), jnp.float32))
        row.append(shifted)
        if part < 3:
            row.append(jnp.zeros((32, REACH - 384 - 128 * part), jnp.float32))
        pieces.append(jnp.concatenate(row, 1))
    filter_hi, filter_lo = split(jnp.concatenate(pieces, 0))
    raw_copy.wait()
    raw = jnp.concatenate([raw_ref[c] for c in range(4)], 0)
    blocks = jnp.concatenate(
        [raw[:, DEC * BLOCK * b : DEC * BLOCK * b + REACH] for b in range(TD // BLOCK)], 0
    )
    raw_hi, raw_lo = split(blocks)
    sums = product_nt(
        jnp.concatenate([raw_hi, raw_lo], 0), jnp.concatenate([filter_hi, filter_lo], 0)
    )
    count = 8 * (TD // BLOCK)
    sums = sums[:count, :BLOCK] + (
        sums[count:, :BLOCK] + sums[:count, BLOCK:] + sums[count:, BLOCK:]
    )
    for b in range(TD // BLOCK):
        pad_ref[8:16, BLOCK * b : BLOCK * (b + 1)] = sums[8 * b : 8 * b + 8]

    pl.semaphore_wait(barrier, n - 1)

    to_right = pltpu.make_async_remote_copy(
        src_ref=pad_ref.at[8:16],
        dst_ref=pad_ref.at[0:8],
        send_sem=halo_send.at[0],
        recv_sem=halo_recv.at[0],
        device_id={"chan": lax.rem(me + 1, n)},
        device_id_type=MESH,
    )
    to_left = pltpu.make_async_remote_copy(
        src_ref=pad_ref.at[8:16],
        dst_ref=pad_ref.at[16:24],
        send_sem=halo_send.at[1],
        recv_sem=halo_recv.at[1],
        device_id={"chan": lax.rem(me + n - 1, n)},
        device_id_type=MESH,
    )

    @pl.when(me < n - 1)
    def _():
        to_right.start()

    @pl.when(me > 0)
    def _():
        to_left.start()

    masks = []
    keep_copy.wait()
    keep = jnp.broadcast_to(keep_ref[...].astype(jnp.float32), (16 * COLS, total_ch))
    row = lax.broadcasted_iota(jnp.int32, keep.shape, 0)
    dist = lax.broadcasted_iota(jnp.int32, keep.shape, 1)
    for chunk in range(n // COLS):
        gap = jnp.abs(4 * me + row // (4 * COLS) - (row % (4 * COLS) + chunk * 4 * COLS))
        hit = jnp.where((gap == dist) & (dist > 0), keep, 0.0)
        masks.append(jnp.sum(hit, axis=1, keepdims=True))
    taps_copy.wait()
    flags_copy.wait()

    @pl.when(me > 0)
    def _():
        to_right.wait_recv()

    @pl.when(me == 0)
    def _():
        pad_ref[0:8] = jnp.zeros((8, TD), jnp.float32)

    @pl.when(me < n - 1)
    def _():
        to_left.wait_recv()

    @pl.when(me == n - 1)
    def _():
        pad_ref[16:24] = jnp.zeros((8, TD), jnp.float32)

    filtered = taps_ref[0] * pad_ref[0:8]
    for offset in range(1, SPAN):
        filtered = filtered + taps_ref[offset] * pad_ref[2 * offset : 2 * offset + 8]
    for tile in range(TD // 128):
        filt_ref[8 * tile : 8 * tile + 8] = filtered[:, 128 * tile : 128 * (tile + 1)]
    for s in range(S):
        for tile in range(TD // 128):
            one = filt_ref[pl.ds(8 * tile + s, 4, stride=2), :]
            dup_ref[8 * s : 8 * s + 4, 128 * tile : 128 * (tile + 1)] = one
            dup_ref[8 * s + 4 : 8 * s + 8, 128 * tile : 128 * (tile + 1)] = one
    windows = jnp.concatenate(
        [dup_ref[8 * s : 8 * s + 8, NT * w : NT * (w + 1)] for s in range(S) for w in range(W)], 0
    )
    win_hi, win_lo = split(windows)
    dft_copy.wait()
    spectra = jnp.dot(
        jnp.concatenate([win_hi, win_lo], 0), dft_ref[...], preferred_element_type=jnp.float32
    )
    spectra = spectra[:ROWS, : 2 * NF] + (
        spectra[ROWS:, : 2 * NF] + spectra[:ROWS, 2 * NF :] + spectra[ROWS:, 2 * NF :]
    )
    real, imag = spectra[:, :NF], spectra[:, NF:]
    rows = lax.broadcasted_iota(jnp.int32, (ROWS, NF), 0)
    lanes = lax.broadcasted_iota(jnp.int32, (ROWS, NF), 1)
    flag = jnp.zeros((ROWS, NF), jnp.float32)
    for s in range(S):
        for c in range(4):
            here = (rows // 16 == s) & (rows % 4 == c)
            flag = jnp.where(here, flags_ref[s, c].astype(jnp.float32), flag)
    factor = flag / jnp.maximum(jnp.sqrt(real * real + imag * imag), 0.25)
    is_real = (rows // 4) % 2 == 0
    real = (real * factor).astype(jnp.bfloat16).astype(jnp.float32)
    imag = (imag * factor).astype(jnp.bfloat16).astype(jnp.float32)
    stash = (lanes == 0) & (~is_real)
    spec = jnp.where(is_real, real, imag)
    all_ref[me] = jnp.where(stash, flag, spec).astype(jnp.bfloat16)

    def copy_to(k):
        return pltpu.make_async_remote_copy(
            src_ref=all_ref.at[me],
            dst_ref=all_ref.at[me],
            send_sem=send_sem.at[k],
            recv_sem=recv_sem.at[me],
            device_id={"chan": lax.rem(me + k, n)},
            device_id_type=MESH,
        )

    def send(k, carry):
        copy_to(k).start()
        return carry

    lax.fori_loop(1, n, send, 0)

    spec_ref[...] = jnp.where(stash, 0.0, spec)
    turn_ref[...] = jnp.where(stash, flag, jnp.where(is_real, imag, -real))
    upper = lax.broadcasted_iota(jnp.int32, (8, NF), 0) < 4
    for ref, target in ((spec_ref, own_ref), (turn_ref, own_turn_ref)):
        for i in range(4):
            for k in range(S * W):
                first = jnp.broadcast_to(ref[8 * k + i : 8 * k + i + 1], (8, NF))
                second = jnp.broadcast_to(ref[8 * k + 4 + i : 8 * k + 5 + i], (8, NF))
                target[i, 8 * k : 8 * k + 8] = jnp.where(upper, first, second)
    lag_copy.wait()

    def receive(k, carry):
        src = lax.rem(me + k, n)
        pltpu.make_async_remote_copy(
            src_ref=all_ref.at[src],
            dst_ref=all_ref.at[src],
            send_sem=send_sem.at[k],
            recv_sem=recv_sem.at[src],
            device_id={"chan": src},
            device_id_type=MESH,
        ).wait_recv()
        return carry

    lax.fori_loop(1, n, receive, 0)

    for chunk in range(n // COLS):

        def quad(q, carry):
            base = chunk * COLS + 4 * q
            for i in range(4):
                for half, ref in enumerate((own_ref, own_turn_ref)):
                    sums = []
                    for d in range(4):
                        theirs = all_ref[base + d].astype(jnp.float32)
                        acc = ref[i, 0:8] * theirs[0:8]
                        for k in range(1, S * W):
                            acc = acc + ref[i, 8 * k : 8 * k + 8] * theirs[8 * k : 8 * k + 8]
                        sums.append(acc)
                    both = []
                    for d in (0, 2):
                        a, b = sums[d], sums[d + 1]
                        both.append(
                            jnp.where(upper, a, b) + pltpu.roll(jnp.where(upper, b, a), 4, 0)
                        )
                    high, low = split(jnp.concatenate(both, 0))
                    at = pl.ds(pl.multiple_of(4 * COLS * i + 16 * q, 16), 16)
                    cross_hi_ref[at, NF * half : NF * (half + 1)] = high
                    cross_lo_ref[at, NF * half : NF * (half + 1)] = low
            return carry

        lax.fori_loop(0, COLS // 4, quad, 0)
        lag = lag_ref[...]
        summed = product_nt(cross_hi_ref[...], lag)
        summed = (
            summed[:, :LAG_ROWS]
            + summed[:, LAG_ROWS:]
            + product_nt(cross_lo_ref[...], lag[:LAG_ROWS])
        )
        scale = masks[chunk] / jnp.maximum(summed[:, LAGS : LAGS + 1], 1.0)
        result = (summed * scale).astype(jnp.bfloat16)
        for i in range(4):
            out_ref[i, 4 * COLS * chunk : 4 * COLS * (chunk + 1), :] = result[
                4 * COLS * i : 4 * COLS * (i + 1), :LAGS
            ]

    def sent(k, carry):
        copy_to(k).wait_send()
        return carry

    lax.fori_loop(1, n, sent, 0)

    @pl.when(me < n - 1)
    def _():
        to_right.wait_send()

    @pl.when(me > 0)
    def _():
        to_left.wait_send()


def on_device(raw, fir, spatial_taps, flags, keep):
    n = lax.axis_size("chan")
    vmem = pl.BlockSpec(memory_space=pltpu.VMEM)
    hbm = pl.BlockSpec(memory_space=pltpu.HBM)
    out = pl.pallas_call(
        functools.partial(kernel, n),
        out_shape=jax.ShapeDtypeStruct((4, 4 * n, LAGS), jnp.bfloat16),
        in_specs=[hbm] * 7,
        out_specs=vmem,
        scratch_shapes=[
            pltpu.VMEM(raw.shape, jnp.float32),
            pltpu.VMEM((1, TAPS), jnp.float32),
            pltpu.SMEM((SPAN,), jnp.float32),
            pltpu.SMEM((S, 4), jnp.int32),
            pltpu.VMEM((1, 4 * n), jnp.int32),
            pltpu.VMEM((NT, 4 * NF), jnp.bfloat16),
            pltpu.VMEM((2 * LAG_ROWS, 2 * NF), jnp.bfloat16),
            pltpu.VMEM((32, 384), jnp.float32),
            pltpu.VMEM((24, TD), jnp.float32),
            pltpu.VMEM((TD // 16, 128), jnp.float32),
            pltpu.VMEM((16, TD), jnp.float32),
            pltpu.VMEM((ROWS, NF), jnp.float32),
            pltpu.VMEM((ROWS, NF), jnp.float32),
            pltpu.VMEM((4, ROWS, NF), jnp.float32),
            pltpu.VMEM((4, ROWS, NF), jnp.float32),
            pltpu.VMEM((n, ROWS, NF), jnp.bfloat16),
            pltpu.VMEM((16 * COLS, 2 * NF), jnp.bfloat16),
            pltpu.VMEM((16 * COLS, 2 * NF), jnp.bfloat16),
            pltpu.SemaphoreType.DMA((7,)),
            pltpu.SemaphoreType.DMA((2,)),
            pltpu.SemaphoreType.DMA((2,)),
            pltpu.SemaphoreType.DMA((n,)),
            pltpu.SemaphoreType.DMA((n,)),
        ],
        compiler_params=pltpu.CompilerParams(
            collective_id=0, has_side_effects=True, vmem_limit_bytes=65400 * 1024
        ),
    )(
        raw,
        fir.reshape(1, TAPS),
        spatial_taps,
        flags.T,
        keep.reshape(1, 4 * n),
        jnp.asarray(dft_table()),
        jnp.asarray(lag_table()),
    )
    return jnp.swapaxes(out, 1, 2)


def solution(mesh):
    placed = (P(("groups", "chan"), None, None), P(), P(), P(("groups", "chan"), None), P())
    return jax.shard_map(
        on_device,
        mesh=mesh,
        in_specs=placed,
        out_specs=P(("groups", "chan"), None, None),
        check_vma=False,
    )
```

```python
import functools
import math

import jax
import jax.numpy as jnp
import ml_dtypes
import numpy as np
from jax import lax
from jax.experimental import pallas as pl
from jax.experimental.pallas import tpu as pltpu
from jax.sharding import PartitionSpec as P

S = 2
W = 2
NT = 512
TAPS = 255
DEC = 4
SPAN = 9
LAGS = 101
NF = 256
TD = 1024
HALFLAG = 50
ROWS = 32
LAG_ROWS = 128
BLOCK = 128
REACH = DEC * BLOCK + TAPS + 1
COLS = 16
MESH = pl.DeviceIdType.MESH


def halves(values):
    high = values.astype(ml_dtypes.bfloat16)
    return high, (values - high.astype(np.float64)).astype(ml_dtypes.bfloat16)


def dft_table():
    time = np.arange(NT)
    angles = (time[:, None] * np.arange(NF)[None, :] % NT) * (2.0 * math.pi / NT)
    taper = (0.5 - 0.5 * np.cos(time * (2.0 * math.pi / NT))) / math.sqrt(NT)
    sine = -np.sin(angles)
    sine[:, 0] = 0.0
    table = np.concatenate([np.cos(angles), sine], 1) * taper[:, None]
    return np.concatenate(halves(table), 1)


def lag_table():
    freq = np.arange(NF)
    lags = np.arange(LAGS) - HALFLAG
    angles = (lags[:, None] * freq[None, :] % NT) * (2.0 * math.pi / NT)
    one_sided = np.where(freq == 0, 1.0, 2.0) / (2.0 * math.sqrt(NF))
    table = np.zeros((LAG_ROWS, 2 * NF))
    table[:LAGS, :NF] = one_sided * np.cos(angles)
    table[:LAGS, NF:] = -one_sided * np.sin(angles)
    table[:LAGS, NF] = 0.0
    table[LAGS, NF] = 0.5
    return np.concatenate(halves(table), 0)


def split(values):
    high = values.astype(jnp.bfloat16)
    return high, (values - high.astype(jnp.float32)).astype(jnp.bfloat16)


def product_nt(left, right):
    return lax.dot_general(
        left, right, (((1,), (1,)), ((), ())), preferred_element_type=jnp.float32
    )


def kernel(
    n,
    raw_hbm,
    fir_hbm,
    taps_hbm,
    flags_hbm,
    keep_hbm,
    dft_hbm,
    lag_hbm,
    out_ref,
    raw_ref,
    fir_ref,
    taps_ref,
    flags_ref,
    keep_ref,
    dft_ref,
    lag_ref,
    firs_ref,
    pad_ref,
    filt_ref,
    dup_ref,
    spec_ref,
    turn_ref,
    own_ref,
    own_turn_ref,
    all_ref,
    cross_hi_ref,
    cross_lo_ref,
    table_sem,
    halo_send,
    halo_recv,
    send_sem,
    pass_sem,
    recv_sem,
):
    me = lax.axis_index("chan")
    total_ch = 4 * n

    pairs = (
        (fir_hbm, fir_ref),
        (raw_hbm, raw_ref),
        (dft_hbm, dft_ref),
        (taps_hbm, taps_ref),
        (flags_hbm, flags_ref),
        (keep_hbm, keep_ref),
        (lag_hbm, lag_ref),
    )
    copies = [
        pltpu.make_async_copy(src, dst, table_sem.at[k]) for k, (src, dst) in enumerate(pairs)
    ]
    for copy in copies:
        copy.start()
    fir_copy, raw_copy, dft_copy, taps_copy, flags_copy, keep_copy, lag_copy = copies

    barrier = pltpu.get_barrier_semaphore()

    def greet(k, carry):
        peer = lax.rem(me + 2 * k, n)
        pl.semaphore_signal(barrier, inc=1, device_id={"chan": peer}, device_id_type=MESH)
        return carry

    core = lax.rem(me, 2)
    partner = me + 1 - 2 * core
    across = lax.rem(me + n - 1 + 2 * core, n)
    for peer in (partner, across):
        pl.semaphore_signal(barrier, inc=1, device_id={"chan": peer}, device_id_type=MESH)
    lax.fori_loop(1, n // 2, greet, 0)

    firs_ref[...] = jnp.zeros_like(firs_ref)
    fir_copy.wait()
    firs_ref[:, 0:TAPS] = jnp.broadcast_to(fir_ref[...], (32, TAPS))
    shifted = firs_ref[...]
    row_id = lax.broadcasted_iota(jnp.int32, shifted.shape, 0)
    for bit in range(5):
        moved = pltpu.roll(shifted, DEC << bit, 1)
        shifted = jnp.where((row_id // (1 << bit)) % 2 == 1, moved, shifted)
    pieces = []
    for part in range(4):
        row = []
        if part:
            row.append(jnp.zeros((32, 128 * part), jnp.float32))
        row.append(shifted)
        if part < 3:
            row.append(jnp.zeros((32, REACH - 384 - 128 * part), jnp.float32))
        pieces.append(jnp.concatenate(row, 1))
    filter_hi, filter_lo = split(jnp.concatenate(pieces, 0))
    raw_copy.wait()
    raw = jnp.concatenate([raw_ref[c] for c in range(4)], 0)
    blocks = jnp.concatenate(
        [raw[:, DEC * BLOCK * b : DEC * BLOCK * b + REACH] for b in range(TD // BLOCK)], 0
    )
    raw_hi, raw_lo = split(blocks)
    sums = product_nt(
        jnp.concatenate([raw_hi, raw_lo], 0), jnp.concatenate([filter_hi, filter_lo], 0)
    )
    count = 8 * (TD // BLOCK)
    sums = sums[:count, :BLOCK] + (
        sums[count:, :BLOCK] + sums[:count, BLOCK:] + sums[count:, BLOCK:]
    )
    for b in range(TD // BLOCK):
        pad_ref[8:16, BLOCK * b : BLOCK * (b + 1)] = sums[8 * b : 8 * b + 8]

    pl.semaphore_wait(barrier, n // 2 + 1)

    to_right = pltpu.make_async_remote_copy(
        src_ref=pad_ref.at[8:16],
        dst_ref=pad_ref.at[0:8],
        send_sem=halo_send.at[0],
        recv_sem=halo_recv.at[0],
        device_id={"chan": lax.rem(me + 1, n)},
        device_id_type=MESH,
    )
    to_left = pltpu.make_async_remote_copy(
        src_ref=pad_ref.at[8:16],
        dst_ref=pad_ref.at[16:24],
        send_sem=halo_send.at[1],
        recv_sem=halo_recv.at[1],
        device_id={"chan": lax.rem(me + n - 1, n)},
        device_id_type=MESH,
    )

    @pl.when(me < n - 1)
    def _():
        to_right.start()

    @pl.when(me > 0)
    def _():
        to_left.start()

    masks = []
    keep_copy.wait()
    keep = jnp.broadcast_to(keep_ref[...].astype(jnp.float32), (16 * COLS, total_ch))
    row = lax.broadcasted_iota(jnp.int32, keep.shape, 0)
    dist = lax.broadcasted_iota(jnp.int32, keep.shape, 1)
    for chunk in range(n // COLS):
        gap = jnp.abs(4 * me + row // (4 * COLS) - (row % (4 * COLS) + chunk * 4 * COLS))
        hit = jnp.where((gap == dist) & (dist > 0), keep, 0.0)
        masks.append(jnp.sum(hit, axis=1, keepdims=True))
    taps_copy.wait()
    flags_copy.wait()

    @pl.when(me > 0)
    def _():
        to_right.wait_recv()

    @pl.when(me == 0)
    def _():
        pad_ref[0:8] = jnp.zeros((8, TD), jnp.float32)

    @pl.when(me < n - 1)
    def _():
        to_left.wait_recv()

    @pl.when(me == n - 1)
    def _():
        pad_ref[16:24] = jnp.zeros((8, TD), jnp.float32)

    filtered = taps_ref[0] * pad_ref[0:8]
    for offset in range(1, SPAN):
        filtered = filtered + taps_ref[offset] * pad_ref[2 * offset : 2 * offset + 8]
    for tile in range(TD // 128):
        filt_ref[8 * tile : 8 * tile + 8] = filtered[:, 128 * tile : 128 * (tile + 1)]
    for s in range(S):
        for tile in range(TD // 128):
            one = filt_ref[pl.ds(8 * tile + s, 4, stride=2), :]
            dup_ref[8 * s : 8 * s + 4, 128 * tile : 128 * (tile + 1)] = one
            dup_ref[8 * s + 4 : 8 * s + 8, 128 * tile : 128 * (tile + 1)] = one
    windows = jnp.concatenate(
        [dup_ref[8 * s : 8 * s + 8, NT * w : NT * (w + 1)] for s in range(S) for w in range(W)], 0
    )
    win_hi, win_lo = split(windows)
    dft_copy.wait()
    spectra = jnp.dot(
        jnp.concatenate([win_hi, win_lo], 0), dft_ref[...], preferred_element_type=jnp.float32
    )
    spectra = spectra[:ROWS, : 2 * NF] + (
        spectra[ROWS:, : 2 * NF] + spectra[:ROWS, 2 * NF :] + spectra[ROWS:, 2 * NF :]
    )
    real, imag = spectra[:, :NF], spectra[:, NF:]
    rows = lax.broadcasted_iota(jnp.int32, (ROWS, NF), 0)
    lanes = lax.broadcasted_iota(jnp.int32, (ROWS, NF), 1)
    flag = jnp.zeros((ROWS, NF), jnp.float32)
    for s in range(S):
        for c in range(4):
            here = (rows // 16 == s) & (rows % 4 == c)
            flag = jnp.where(here, flags_ref[s, c].astype(jnp.float32), flag)
    factor = flag / jnp.maximum(jnp.sqrt(real * real + imag * imag), 0.25)
    is_real = (rows // 4) % 2 == 0
    real = (real * factor).astype(jnp.bfloat16).astype(jnp.float32)
    imag = (imag * factor).astype(jnp.bfloat16).astype(jnp.float32)
    stash = (lanes == 0) & (~is_real)
    spec = jnp.where(is_real, real, imag)
    all_ref[me] = jnp.where(stash, flag, spec).astype(jnp.bfloat16)

    def copy_block(src, peer, sem):
        return pltpu.make_async_remote_copy(
            src_ref=all_ref.at[src],
            dst_ref=all_ref.at[src],
            send_sem=sem,
            recv_sem=recv_sem.at[src],
            device_id={"chan": peer},
            device_id_type=MESH,
        )

    def own_copy(k):
        return copy_block(me, lax.rem(me + n - 2 * k, n), send_sem.at[k])

    def send(k, carry):
        own_copy(k).start()
        return carry

    copy_block(me, partner, send_sem.at[0]).start()
    lax.fori_loop(1, n // 2, send, 0)

    spec_ref[...] = jnp.where(stash, 0.0, spec)
    turn_ref[...] = jnp.where(stash, flag, jnp.where(is_real, imag, -real))
    upper = lax.broadcasted_iota(jnp.int32, (8, NF), 0) < 4
    for ref, target in ((spec_ref, own_ref), (turn_ref, own_turn_ref)):
        for i in range(4):
            for k in range(S * W):
                first = jnp.broadcast_to(ref[8 * k + i : 8 * k + i + 1], (8, NF))
                second = jnp.broadcast_to(ref[8 * k + 4 + i : 8 * k + 5 + i], (8, NF))
                target[i, 8 * k : 8 * k + 8] = jnp.where(upper, first, second)
    lag_copy.wait()

    def pass_on(plane):
        for chip in range(2):
            src = 4 * plane + 2 * chip + core

            @pl.when(src != me)
            def _():
                copy_block(src, partner, pass_sem.at[src]).wait_recv()
                copy_block(src, partner, pass_sem.at[src]).start()

    quads = COLS // 4
    for chunk in range(n // COLS):

        def local_of(q):
            return lax.rem(me // 4 + q, quads)

        pass_on(chunk * quads + local_of(0))

        def quad(q, carry):
            local = local_of(q)

            @pl.when(q < quads - 1)
            def _():
                pass_on(chunk * quads + local_of(q + 1))

            base = chunk * COLS + 4 * local
            for chip in range(2):
                src = base + 2 * chip + 1 - core
                copy_block(src, partner, pass_sem.at[src]).wait_recv()
            for i in range(4):
                for half, ref in enumerate((own_ref, own_turn_ref)):
                    sums = []
                    for d in range(4):
                        theirs = all_ref[base + d].astype(jnp.float32)
                        acc = ref[i, 0:8] * theirs[0:8]
                        for k in range(1, S * W):
                            acc = acc + ref[i, 8 * k : 8 * k + 8] * theirs[8 * k : 8 * k + 8]
                        sums.append(acc)
                    both = []
                    for d in (0, 2):
                        a, b = sums[d], sums[d + 1]
                        both.append(
                            jnp.where(upper, a, b) + pltpu.roll(jnp.where(upper, b, a), 4, 0)
                        )
                    high, low = split(jnp.concatenate(both, 0))
                    at = pl.ds(pl.multiple_of(4 * COLS * i + 16 * local, 16), 16)
                    cross_hi_ref[at, NF * half : NF * (half + 1)] = high
                    cross_lo_ref[at, NF * half : NF * (half + 1)] = low
            return carry

        lax.fori_loop(0, quads, quad, 0)
        lag = lag_ref[...]
        summed = product_nt(cross_hi_ref[...], lag)
        summed = (
            summed[:, :LAG_ROWS]
            + summed[:, LAG_ROWS:]
            + product_nt(cross_lo_ref[...], lag[:LAG_ROWS])
        )
        scale = masks[chunk] / jnp.maximum(summed[:, LAGS : LAGS + 1], 1.0)
        result = (summed * scale).astype(jnp.bfloat16)
        for i in range(4):
            out_ref[i, 4 * COLS * chunk : 4 * COLS * (chunk + 1), :] = result[
                4 * COLS * i : 4 * COLS * (i + 1), :LAGS
            ]

    copy_block(me, partner, send_sem.at[0]).wait_send()

    def sent(k, carry):
        own_copy(k).wait_send()
        src = lax.rem(me + 2 * k, n)
        copy_block(src, partner, pass_sem.at[src]).wait_send()
        return carry

    lax.fori_loop(1, n // 2, sent, 0)

    @pl.when(me < n - 1)
    def _():
        to_right.wait_send()

    @pl.when(me > 0)
    def _():
        to_left.wait_send()


def on_device(raw, fir, spatial_taps, flags, keep):
    n = lax.axis_size("chan")
    vmem = pl.BlockSpec(memory_space=pltpu.VMEM)
    hbm = pl.BlockSpec(memory_space=pltpu.HBM)
    out = pl.pallas_call(
        functools.partial(kernel, n),
        out_shape=pltpu.VMEM((4, 4 * n, LAGS), jnp.bfloat16),
        in_specs=[hbm] * 7,
        out_specs=vmem,
        scratch_shapes=[
            pltpu.VMEM(raw.shape, jnp.float32),
            pltpu.VMEM((1, TAPS), jnp.float32),
            pltpu.SMEM((SPAN,), jnp.float32),
            pltpu.SMEM((S, 4), jnp.int32),
            pltpu.VMEM((1, 4 * n), jnp.int32),
            pltpu.VMEM((NT, 4 * NF), jnp.bfloat16),
            pltpu.VMEM((2 * LAG_ROWS, 2 * NF), jnp.bfloat16),
            pltpu.VMEM((32, 384), jnp.float32),
            pltpu.VMEM((24, TD), jnp.float32),
            pltpu.VMEM((TD // 16, 128), jnp.float32),
            pltpu.VMEM((16, TD), jnp.float32),
            pltpu.VMEM((ROWS, NF), jnp.float32),
            pltpu.VMEM((ROWS, NF), jnp.float32),
            pltpu.VMEM((4, ROWS, NF), jnp.float32),
            pltpu.VMEM((4, ROWS, NF), jnp.float32),
            pltpu.VMEM((n, ROWS, NF), jnp.bfloat16),
            pltpu.VMEM((16 * COLS, 2 * NF), jnp.bfloat16),
            pltpu.VMEM((16 * COLS, 2 * NF), jnp.bfloat16),
            pltpu.SemaphoreType.DMA((7,)),
            pltpu.SemaphoreType.DMA((2,)),
            pltpu.SemaphoreType.DMA((2,)),
            pltpu.SemaphoreType.DMA((n // 2,)),
            pltpu.SemaphoreType.DMA((n,)),
            pltpu.SemaphoreType.DMA((n,)),
        ],
        compiler_params=pltpu.CompilerParams(
            collective_id=0, has_side_effects=True, vmem_limit_bytes=48 * 2**20
        ),
    )(
        *[
            pltpu.with_memory_space_constraint(value, pltpu.HBM)
            for value in (
                raw,
                fir.reshape(1, TAPS),
                spatial_taps,
                flags.T,
                keep.reshape(1, 4 * n),
                jnp.asarray(dft_table()),
                jnp.asarray(lag_table()),
            )
        ]
    )
    return jnp.swapaxes(out, 1, 2)


def solution(mesh):
    placed = (P(("groups", "chan"), None, None), P(), P(), P(("groups", "chan"), None), P())
    return jax.shard_map(
        on_device,
        mesh=mesh,
        in_specs=placed,
        out_specs=P(("groups", "chan"), None, None),
        check_vma=False,
    )
```

```python
import functools
import math

import jax
import jax.numpy as jnp
import ml_dtypes
import numpy as np
from jax import lax
from jax.experimental import pallas as pl
from jax.experimental.pallas import tpu as pltpu
from jax.sharding import PartitionSpec as P

S = 2
W = 2
NT = 512
TAPS = 255
DEC = 4
SPAN = 9
LAGS = 101
NF = 256
TD = 1024
HALFLAG = 50
ROWS = 32
LAG_ROWS = 128
BLOCK = 128
REACH = DEC * BLOCK + TAPS + 1
COLS = 16
MESH = pl.DeviceIdType.MESH


def halves(values):
    high = values.astype(ml_dtypes.bfloat16)
    return high, (values - high.astype(np.float64)).astype(ml_dtypes.bfloat16)


def dft_table():
    time = np.arange(NT)
    angles = (time[:, None] * np.arange(NF)[None, :] % NT) * (2.0 * math.pi / NT)
    taper = (0.5 - 0.5 * np.cos(time * (2.0 * math.pi / NT))) / math.sqrt(NT)
    sine = -np.sin(angles)
    sine[:, 0] = 0.0
    table = np.concatenate([np.cos(angles), sine], 1) * taper[:, None]
    return np.concatenate(halves(table), 1)


def lag_table():
    freq = np.arange(NF)
    lags = np.arange(LAGS) - HALFLAG
    angles = (lags[:, None] * freq[None, :] % NT) * (2.0 * math.pi / NT)
    one_sided = np.where(freq == 0, 1.0, 2.0) / (2.0 * math.sqrt(NF))
    table = np.zeros((LAG_ROWS, 2 * NF))
    table[:LAGS, :NF] = one_sided * np.cos(angles)
    table[:LAGS, NF:] = -one_sided * np.sin(angles)
    table[:LAGS, NF] = 0.0
    table[LAGS, NF] = 0.5
    return np.concatenate(halves(table), 0)


def split(values):
    high = values.astype(jnp.bfloat16)
    return high, (values - high.astype(jnp.float32)).astype(jnp.bfloat16)


def product_nt(left, right):
    return lax.dot_general(
        left, right, (((1,), (1,)), ((), ())), preferred_element_type=jnp.float32
    )


def kernel(
    n,
    raw_hbm,
    fir_hbm,
    taps_hbm,
    flags_hbm,
    keep_hbm,
    dft_hbm,
    lag_hbm,
    out_ref,
    raw_ref,
    fir_ref,
    taps_ref,
    flags_ref,
    keep_ref,
    dft_ref,
    lag_ref,
    firs_ref,
    pad_ref,
    filt_ref,
    dup_ref,
    spec_ref,
    turn_ref,
    own_ref,
    own_turn_ref,
    all_ref,
    cross_hi_ref,
    cross_lo_ref,
    table_sem,
    halo_send,
    halo_recv,
    send_sem,
    pass_sem,
    recv_sem,
):
    me = lax.axis_index("chan")
    total_ch = 4 * n

    pairs = (
        (fir_hbm, fir_ref),
        (raw_hbm, raw_ref),
        (dft_hbm, dft_ref),
        (taps_hbm, taps_ref),
        (flags_hbm, flags_ref),
        (keep_hbm, keep_ref),
        (lag_hbm, lag_ref),
    )
    copies = [
        pltpu.make_async_copy(src, dst, table_sem.at[k]) for k, (src, dst) in enumerate(pairs)
    ]
    for copy in copies:
        copy.start()
    fir_copy, raw_copy, dft_copy, taps_copy, flags_copy, keep_copy, lag_copy = copies

    barrier = pltpu.get_barrier_semaphore()

    def greet(k, carry):
        peer = lax.rem(me + 2 * k, n)
        pl.semaphore_signal(barrier, inc=1, device_id={"chan": peer}, device_id_type=MESH)
        return carry

    core = lax.rem(me, 2)
    partner = me + 1 - 2 * core
    across = lax.rem(me + n - 1 + 2 * core, n)
    for peer in (partner, across):
        pl.semaphore_signal(barrier, inc=1, device_id={"chan": peer}, device_id_type=MESH)
    lax.fori_loop(1, n // 2, greet, 0)

    firs_ref[...] = jnp.zeros_like(firs_ref)
    fir_copy.wait()
    firs_ref[:, 0:TAPS] = jnp.broadcast_to(fir_ref[...], (32, TAPS))
    shifted = firs_ref[...]
    row_id = lax.broadcasted_iota(jnp.int32, shifted.shape, 0)
    for bit in range(5):
        moved = pltpu.roll(shifted, DEC << bit, 1)
        shifted = jnp.where((row_id // (1 << bit)) % 2 == 1, moved, shifted)
    pieces = []
    for part in range(4):
        row = []
        if part:
            row.append(jnp.zeros((32, 128 * part), jnp.float32))
        row.append(shifted)
        if part < 3:
            row.append(jnp.zeros((32, REACH - 384 - 128 * part), jnp.float32))
        pieces.append(jnp.concatenate(row, 1))
    filter_hi, filter_lo = split(jnp.concatenate(pieces, 0))
    raw_copy.wait()
    raw = jnp.concatenate([raw_ref[c] for c in range(4)], 0)
    blocks = jnp.concatenate(
        [raw[:, DEC * BLOCK * b : DEC * BLOCK * b + REACH] for b in range(TD // BLOCK)], 0
    )
    raw_hi, raw_lo = split(blocks)
    sums = product_nt(
        jnp.concatenate([raw_hi, raw_lo], 0), jnp.concatenate([filter_hi, filter_lo], 0)
    )
    count = 8 * (TD // BLOCK)
    sums = sums[:count, :BLOCK] + (
        sums[count:, :BLOCK] + sums[:count, BLOCK:] + sums[count:, BLOCK:]
    )
    per = NT // BLOCK
    windows = jnp.concatenate(
        [
            jnp.concatenate([sums[8 * b : 8 * b + 8] for b in range(per * w, per * (w + 1))], 1)
            for w in range(W)
        ],
        0,
    )
    win_hi, win_lo = split(windows)
    dft_copy.wait()
    spectra = jnp.dot(
        jnp.concatenate([win_hi, win_lo], 0), dft_ref[...], preferred_element_type=jnp.float32
    )
    half = 8 * W
    spectra = spectra[:half, : 2 * NF] + (
        spectra[half:, : 2 * NF] + spectra[:half, 2 * NF :] + spectra[half:, 2 * NF :]
    )
    for w in range(W):
        pad_ref[w, 8:16] = spectra[8 * w : 8 * w + 8]

    pl.semaphore_wait(barrier, n // 2 + 1)

    to_right = pltpu.make_async_remote_copy(
        src_ref=pad_ref.at[:, 8:16],
        dst_ref=pad_ref.at[:, 0:8],
        send_sem=halo_send.at[0],
        recv_sem=halo_recv.at[0],
        device_id={"chan": lax.rem(me + 1, n)},
        device_id_type=MESH,
    )
    to_left = pltpu.make_async_remote_copy(
        src_ref=pad_ref.at[:, 8:16],
        dst_ref=pad_ref.at[:, 16:24],
        send_sem=halo_send.at[1],
        recv_sem=halo_recv.at[1],
        device_id={"chan": lax.rem(me + n - 1, n)},
        device_id_type=MESH,
    )

    @pl.when(me < n - 1)
    def _():
        to_right.start()

    @pl.when(me > 0)
    def _():
        to_left.start()

    masks = []
    keep_copy.wait()
    keep = jnp.broadcast_to(keep_ref[...].astype(jnp.float32), (16 * COLS, total_ch))
    row = lax.broadcasted_iota(jnp.int32, keep.shape, 0)
    dist = lax.broadcasted_iota(jnp.int32, keep.shape, 1)
    for chunk in range(n // COLS):
        gap = jnp.abs(4 * me + row // (4 * COLS) - (row % (4 * COLS) + chunk * 4 * COLS))
        hit = jnp.where((gap == dist) & (dist > 0), keep, 0.0)
        masks.append(jnp.sum(hit, axis=1, keepdims=True))
    taps_copy.wait()
    flags_copy.wait()
    rows = lax.broadcasted_iota(jnp.int32, (ROWS, NF), 0)
    lanes = lax.broadcasted_iota(jnp.int32, (ROWS, NF), 1)
    flag = jnp.zeros((ROWS, NF), jnp.float32)
    for s in range(S):
        for c in range(4):
            here = (rows // 16 == s) & (rows % 4 == c)
            flag = jnp.where(here, flags_ref[s, c].astype(jnp.float32), flag)

    @pl.when(me > 0)
    def _():
        to_right.wait_recv()

    @pl.when(me == 0)
    def _():
        pad_ref[:, 0:8] = jnp.zeros((W, 8, 2 * NF), jnp.float32)

    @pl.when(me < n - 1)
    def _():
        to_left.wait_recv()

    @pl.when(me == n - 1)
    def _():
        pad_ref[:, 16:24] = jnp.zeros((W, 8, 2 * NF), jnp.float32)

    for w in range(W):
        filtered = taps_ref[0] * pad_ref[w, 0:8]
        for offset in range(1, SPAN):
            filtered = filtered + taps_ref[offset] * pad_ref[w, 2 * offset : 2 * offset + 8]
        tiles = 2 * NF // 128
        for tile in range(tiles):
            at = 8 * (tiles * w + tile)
            filt_ref[at : at + 8] = filtered[:, 128 * tile : 128 * (tile + 1)]
            for s in range(S):
                one = filt_ref[pl.ds(at + s, 4, stride=2), :]
                row = 8 * (W * s + w)
                dup_ref[row : row + 4, 128 * tile : 128 * (tile + 1)] = one
                dup_ref[row + 4 : row + 8, 128 * tile : 128 * (tile + 1)] = one
    spectra = dup_ref[...]
    real, imag = spectra[:, :NF], spectra[:, NF:]
    factor = flag / jnp.maximum(jnp.sqrt(real * real + imag * imag), 0.25)
    is_real = (rows // 4) % 2 == 0
    real = (real * factor).astype(jnp.bfloat16).astype(jnp.float32)
    imag = (imag * factor).astype(jnp.bfloat16).astype(jnp.float32)
    stash = (lanes == 0) & (~is_real)
    spec = jnp.where(is_real, real, imag)
    all_ref[me] = jnp.where(stash, flag, spec).astype(jnp.bfloat16)

    def copy_block(src, peer, sem):
        return pltpu.make_async_remote_copy(
            src_ref=all_ref.at[src],
            dst_ref=all_ref.at[src],
            send_sem=sem,
            recv_sem=recv_sem.at[src],
            device_id={"chan": peer},
            device_id_type=MESH,
        )

    def own_copy(k):
        return copy_block(me, lax.rem(me + 2 * k, n), send_sem.at[k])

    def send(k, carry):
        own_copy(k).start()
        return carry

    copy_block(me, partner, send_sem.at[0]).start()
    lax.fori_loop(1, n // 2, send, 0)

    spec_ref[...] = jnp.where(stash, 0.0, spec)
    turn_ref[...] = jnp.where(stash, flag, jnp.where(is_real, imag, -real))
    upper = lax.broadcasted_iota(jnp.int32, (8, NF), 0) < 4
    for ref, target in ((spec_ref, own_ref), (turn_ref, own_turn_ref)):
        for i in range(4):
            for k in range(S * W):
                first = jnp.broadcast_to(ref[8 * k + i : 8 * k + i + 1], (8, NF))
                second = jnp.broadcast_to(ref[8 * k + 4 + i : 8 * k + 5 + i], (8, NF))
                target[i, 8 * k : 8 * k + 8] = jnp.where(upper, first, second)
    lag_copy.wait()

    def pass_on(plane):
        for chip in range(2):
            src = 4 * plane + 2 * chip + core

            @pl.when(src != me)
            def _():
                copy_block(src, partner, pass_sem.at[src]).wait_recv()
                copy_block(src, partner, pass_sem.at[src]).start()

    quads = COLS // 4
    for chunk in range(n // COLS):

        def local_of(q):
            return lax.rem(me // 4 + quads - q, quads)

        pass_on(chunk * quads + local_of(0))

        def quad(q, carry):
            local = local_of(q)

            @pl.when(q < quads - 1)
            def _():
                pass_on(chunk * quads + local_of(q + 1))

            base = chunk * COLS + 4 * local
            for chip in range(2):
                src = base + 2 * chip + 1 - core
                copy_block(src, partner, pass_sem.at[src]).wait_recv()
            for i in range(4):
                for half, ref in enumerate((own_ref, own_turn_ref)):
                    sums = []
                    for d in range(4):
                        theirs = all_ref[base + d].astype(jnp.float32)
                        acc = ref[i, 0:8] * theirs[0:8]
                        for k in range(1, S * W):
                            acc = acc + ref[i, 8 * k : 8 * k + 8] * theirs[8 * k : 8 * k + 8]
                        sums.append(acc)
                    both = []
                    for d in (0, 2):
                        a, b = sums[d], sums[d + 1]
                        both.append(
                            jnp.where(upper, a, b) + pltpu.roll(jnp.where(upper, b, a), 4, 0)
                        )
                    high, low = split(jnp.concatenate(both, 0))
                    at = pl.ds(pl.multiple_of(4 * COLS * i + 16 * local, 16), 16)
                    cross_hi_ref[at, NF * half : NF * (half + 1)] = high
                    cross_lo_ref[at, NF * half : NF * (half + 1)] = low
            return carry

        lax.fori_loop(0, quads, quad, 0)
        lag = lag_ref[...]
        summed = product_nt(cross_hi_ref[...], lag)
        summed = (
            summed[:, :LAG_ROWS]
            + summed[:, LAG_ROWS:]
            + product_nt(cross_lo_ref[...], lag[:LAG_ROWS])
        )
        scale = masks[chunk] / jnp.maximum(summed[:, LAGS : LAGS + 1], 1.0)
        result = (summed * scale).astype(jnp.bfloat16)
        for i in range(4):
            out_ref[i, 4 * COLS * chunk : 4 * COLS * (chunk + 1), :] = result[
                4 * COLS * i : 4 * COLS * (i + 1), :LAGS
            ]

    copy_block(me, partner, send_sem.at[0]).wait_send()

    def sent(k, carry):
        own_copy(k).wait_send()
        src = lax.rem(me + 2 * k, n)
        copy_block(src, partner, pass_sem.at[src]).wait_send()
        return carry

    lax.fori_loop(1, n // 2, sent, 0)

    @pl.when(me < n - 1)
    def _():
        to_right.wait_send()

    @pl.when(me > 0)
    def _():
        to_left.wait_send()


def on_device(raw, fir, spatial_taps, flags, keep):
    n = lax.axis_size("chan")
    vmem = pl.BlockSpec(memory_space=pltpu.VMEM)
    hbm = pl.BlockSpec(memory_space=pltpu.HBM)
    out = pl.pallas_call(
        functools.partial(kernel, n),
        out_shape=pltpu.VMEM((4, 4 * n, LAGS), jnp.bfloat16),
        in_specs=[hbm] * 7,
        out_specs=vmem,
        scratch_shapes=[
            pltpu.VMEM(raw.shape, jnp.float32),
            pltpu.VMEM((1, TAPS), jnp.float32),
            pltpu.SMEM((SPAN,), jnp.float32),
            pltpu.SMEM((S, 4), jnp.int32),
            pltpu.VMEM((1, 4 * n), jnp.int32),
            pltpu.VMEM((NT, 4 * NF), jnp.bfloat16),
            pltpu.VMEM((2 * LAG_ROWS, 2 * NF), jnp.bfloat16),
            pltpu.VMEM((32, 384), jnp.float32),
            pltpu.VMEM((W, 24, 2 * NF), jnp.float32),
            pltpu.VMEM((TD // 16, 128), jnp.float32),
            pltpu.VMEM((ROWS, 2 * NF), jnp.float32),
            pltpu.VMEM((ROWS, NF), jnp.float32),
            pltpu.VMEM((ROWS, NF), jnp.float32),
            pltpu.VMEM((4, ROWS, NF), jnp.float32),
            pltpu.VMEM((4, ROWS, NF), jnp.float32),
            pltpu.VMEM((n, ROWS, NF), jnp.bfloat16),
            pltpu.VMEM((16 * COLS, 2 * NF), jnp.bfloat16),
            pltpu.VMEM((16 * COLS, 2 * NF), jnp.bfloat16),
            pltpu.SemaphoreType.DMA((7,)),
            pltpu.SemaphoreType.DMA((2,)),
            pltpu.SemaphoreType.DMA((2,)),
            pltpu.SemaphoreType.DMA((n // 2,)),
            pltpu.SemaphoreType.DMA((n,)),
            pltpu.SemaphoreType.DMA((n,)),
        ],
        compiler_params=pltpu.CompilerParams(
            collective_id=0, has_side_effects=True, vmem_limit_bytes=48 * 2**20
        ),
    )(
        *[
            pltpu.with_memory_space_constraint(value, pltpu.HBM)
            for value in (
                raw,
                fir.reshape(1, TAPS),
                spatial_taps,
                flags.T,
                keep.reshape(1, 4 * n),
                jnp.asarray(dft_table()),
                jnp.asarray(lag_table()),
            )
        ]
    )
    return jnp.swapaxes(out, 1, 2)


def solution(mesh):
    placed = (P(("groups", "chan"), None, None), P(), P(), P(("groups", "chan"), None), P())
    return jax.shard_map(
        on_device,
        mesh=mesh,
        in_specs=placed,
        out_specs=P(("groups", "chan"), None, None),
        check_vma=False,
    )
```

```python
import functools
import math

import jax
import jax.numpy as jnp
import ml_dtypes
import numpy as np
from jax import lax
from jax.experimental import pallas as pl
from jax.experimental.pallas import tpu as pltpu
from jax.sharding import PartitionSpec as P

S = 2
W = 2
NT = 512
TAPS = 255
DEC = 4
SPAN = 9
LAGS = 101
NF = 256
TD = 1024
HALFLAG = 50
ROWS = 32
LAG_ROWS = 128
BLOCK = 128
REACH = DEC * BLOCK + TAPS + 1
COLS = 16
MESH = pl.DeviceIdType.MESH


def halves(values):
    high = values.astype(ml_dtypes.bfloat16)
    return high, (values - high.astype(np.float64)).astype(ml_dtypes.bfloat16)


def dft_table():
    time = np.arange(NT)
    angles = (time[:, None] * np.arange(NF)[None, :] % NT) * (2.0 * math.pi / NT)
    taper = (0.5 - 0.5 * np.cos(time * (2.0 * math.pi / NT))) / math.sqrt(NT)
    sine = -np.sin(angles)
    sine[:, 0] = 0.0
    table = np.concatenate([np.cos(angles), sine], 1) * taper[:, None]
    return np.concatenate(halves(table), 1)


def lag_table():
    freq = np.arange(NF)
    lags = np.arange(LAGS) - HALFLAG
    angles = (lags[:, None] * freq[None, :] % NT) * (2.0 * math.pi / NT)
    one_sided = np.where(freq == 0, 1.0, 2.0) / (2.0 * math.sqrt(NF))
    table = np.zeros((LAG_ROWS, 2 * NF))
    table[:LAGS, :NF] = one_sided * np.cos(angles)
    table[:LAGS, NF:] = -one_sided * np.sin(angles)
    table[:LAGS, NF] = 0.0
    table[LAGS, NF] = 0.5
    return np.concatenate(halves(table), 0)


def split(values):
    high = values.astype(jnp.bfloat16)
    return high, (values - high.astype(jnp.float32)).astype(jnp.bfloat16)


def product_nt(left, right):
    return lax.dot_general(
        left, right, (((1,), (1,)), ((), ())), preferred_element_type=jnp.float32
    )


def kernel(
    n,
    raw_hbm,
    fir_hbm,
    taps_hbm,
    flags_hbm,
    keep_hbm,
    dft_hbm,
    lag_hbm,
    out_ref,
    raw_ref,
    fir_ref,
    taps_ref,
    flags_ref,
    keep_ref,
    dft_ref,
    lag_ref,
    firs_ref,
    pad_ref,
    filt_ref,
    dup_ref,
    spec_ref,
    turn_ref,
    own_ref,
    own_turn_ref,
    all_ref,
    cross_hi_ref,
    cross_lo_ref,
    table_sem,
    halo_send,
    halo_recv,
    send_sem,
    pass_sem,
    recv_sem,
):
    me = lax.axis_index("chan")
    total_ch = 4 * n

    pairs = (
        (fir_hbm, fir_ref),
        (raw_hbm, raw_ref),
        (dft_hbm, dft_ref),
        (taps_hbm, taps_ref),
        (flags_hbm, flags_ref),
        (keep_hbm, keep_ref),
        (lag_hbm, lag_ref),
    )
    copies = [
        pltpu.make_async_copy(src, dst, table_sem.at[k]) for k, (src, dst) in enumerate(pairs)
    ]
    for copy in copies:
        copy.start()
    fir_copy, raw_copy, dft_copy, taps_copy, flags_copy, keep_copy, lag_copy = copies

    barrier = pltpu.get_barrier_semaphore()

    def greet(k, carry):
        peer = lax.rem(me + 2 * k, n)
        pl.semaphore_signal(barrier, inc=1, device_id={"chan": peer}, device_id_type=MESH)
        return carry

    core = lax.rem(me, 2)
    partner = me + 1 - 2 * core
    across = lax.rem(me + n - 1 + 2 * core, n)
    for peer in (partner, across):
        pl.semaphore_signal(barrier, inc=1, device_id={"chan": peer}, device_id_type=MESH)
    lax.fori_loop(1, n // 2, greet, 0, unroll=True)

    firs_ref[...] = jnp.zeros_like(firs_ref)
    fir_copy.wait()
    firs_ref[:, 0:TAPS] = jnp.broadcast_to(fir_ref[...], (32, TAPS))
    shifted = firs_ref[...]
    row_id = lax.broadcasted_iota(jnp.int32, shifted.shape, 0)
    for bit in range(5):
        moved = pltpu.roll(shifted, DEC << bit, 1)
        shifted = jnp.where((row_id // (1 << bit)) % 2 == 1, moved, shifted)
    pieces = []
    for part in range(4):
        row = []
        if part:
            row.append(jnp.zeros((32, 128 * part), jnp.float32))
        row.append(shifted)
        if part < 3:
            row.append(jnp.zeros((32, REACH - 384 - 128 * part), jnp.float32))
        pieces.append(jnp.concatenate(row, 1))
    filter_hi, filter_lo = split(jnp.concatenate(pieces, 0))
    raw_copy.wait()
    raw = jnp.concatenate([raw_ref[c] for c in range(4)], 0)
    blocks = jnp.concatenate(
        [raw[:, DEC * BLOCK * b : DEC * BLOCK * b + REACH] for b in range(TD // BLOCK)], 0
    )
    raw_hi, raw_lo = split(blocks)
    sums = product_nt(
        jnp.concatenate([raw_hi, raw_lo], 0), jnp.concatenate([filter_hi, filter_lo], 0)
    )
    count = 8 * (TD // BLOCK)
    sums = sums[:count, :BLOCK] + (
        sums[count:, :BLOCK] + sums[:count, BLOCK:] + sums[count:, BLOCK:]
    )
    per = NT // BLOCK
    windows = jnp.concatenate(
        [
            jnp.concatenate([sums[8 * b : 8 * b + 8] for b in range(per * w, per * (w + 1))], 1)
            for w in range(W)
        ],
        0,
    )
    win_hi, win_lo = split(windows)
    dft_copy.wait()
    spectra = jnp.dot(
        jnp.concatenate([win_hi, win_lo], 0), dft_ref[...], preferred_element_type=jnp.float32
    )
    half = 8 * W
    spectra = spectra[:half, : 2 * NF] + (
        spectra[half:, : 2 * NF] + spectra[:half, 2 * NF :] + spectra[half:, 2 * NF :]
    )
    for w in range(W):
        pad_ref[w, 8:16] = spectra[8 * w : 8 * w + 8]

    pl.semaphore_wait(barrier, n // 2 + 1)

    to_right = pltpu.make_async_remote_copy(
        src_ref=pad_ref.at[:, 8:16],
        dst_ref=pad_ref.at[:, 0:8],
        send_sem=halo_send.at[0],
        recv_sem=halo_recv.at[0],
        device_id={"chan": lax.rem(me + 1, n)},
        device_id_type=MESH,
    )
    to_left = pltpu.make_async_remote_copy(
        src_ref=pad_ref.at[:, 8:16],
        dst_ref=pad_ref.at[:, 16:24],
        send_sem=halo_send.at[1],
        recv_sem=halo_recv.at[1],
        device_id={"chan": lax.rem(me + n - 1, n)},
        device_id_type=MESH,
    )

    @pl.when(me < n - 1)
    def _():
        to_right.start()

    @pl.when(me > 0)
    def _():
        to_left.start()

    masks = []
    keep_copy.wait()
    keep = jnp.broadcast_to(keep_ref[...].astype(jnp.float32), (16 * COLS, total_ch))
    row = lax.broadcasted_iota(jnp.int32, keep.shape, 0)
    dist = lax.broadcasted_iota(jnp.int32, keep.shape, 1)
    for chunk in range(n // COLS):
        gap = jnp.abs(4 * me + row // (4 * COLS) - (row % (4 * COLS) + chunk * 4 * COLS))
        hit = jnp.where((gap == dist) & (dist > 0), keep, 0.0)
        masks.append(jnp.sum(hit, axis=1, keepdims=True))
    taps_copy.wait()
    flags_copy.wait()
    rows = lax.broadcasted_iota(jnp.int32, (ROWS, NF), 0)
    lanes = lax.broadcasted_iota(jnp.int32, (ROWS, NF), 1)
    flag = jnp.zeros((ROWS, NF), jnp.float32)
    for s in range(S):
        for c in range(4):
            here = (rows // 16 == s) & (rows % 4 == c)
            flag = jnp.where(here, flags_ref[s, c].astype(jnp.float32), flag)

    @pl.when(me > 0)
    def _():
        to_right.wait_recv()

    @pl.when(me == 0)
    def _():
        pad_ref[:, 0:8] = jnp.zeros((W, 8, 2 * NF), jnp.float32)

    @pl.when(me < n - 1)
    def _():
        to_left.wait_recv()

    @pl.when(me == n - 1)
    def _():
        pad_ref[:, 16:24] = jnp.zeros((W, 8, 2 * NF), jnp.float32)

    for w in range(W):
        filtered = taps_ref[0] * pad_ref[w, 0:8]
        for offset in range(1, SPAN):
            filtered = filtered + taps_ref[offset] * pad_ref[w, 2 * offset : 2 * offset + 8]
        tiles = 2 * NF // 128
        for tile in range(tiles):
            at = 8 * (tiles * w + tile)
            filt_ref[at : at + 8] = filtered[:, 128 * tile : 128 * (tile + 1)]
            for s in range(S):
                one = filt_ref[pl.ds(at + s, 4, stride=2), :]
                row = 8 * (W * s + w)
                dup_ref[row : row + 4, 128 * tile : 128 * (tile + 1)] = one
                dup_ref[row + 4 : row + 8, 128 * tile : 128 * (tile + 1)] = one
    spectra = dup_ref[...]
    real, imag = spectra[:, :NF], spectra[:, NF:]
    factor = flag / jnp.maximum(jnp.sqrt(real * real + imag * imag), 0.25)
    is_real = (rows // 4) % 2 == 0
    real = (real * factor).astype(jnp.bfloat16).astype(jnp.float32)
    imag = (imag * factor).astype(jnp.bfloat16).astype(jnp.float32)
    stash = (lanes == 0) & (~is_real)
    spec = jnp.where(is_real, real, imag)
    all_ref[me] = jnp.where(stash, flag, spec).astype(jnp.bfloat16)

    def copy_block(src, peer, sem):
        return pltpu.make_async_remote_copy(
            src_ref=all_ref.at[src],
            dst_ref=all_ref.at[src],
            send_sem=sem,
            recv_sem=recv_sem.at[src],
            device_id={"chan": peer},
            device_id_type=MESH,
        )

    def own_copy(k):
        return copy_block(me, lax.rem(me + 2 * k, n), send_sem.at[k])

    def send(k, carry):
        own_copy(k).start()
        return carry

    copy_block(me, partner, send_sem.at[0]).start()
    lax.fori_loop(1, n // 2, send, 0, unroll=True)

    spec_ref[...] = jnp.where(stash, 0.0, spec)
    turn_ref[...] = jnp.where(stash, flag, jnp.where(is_real, imag, -real))
    upper = lax.broadcasted_iota(jnp.int32, (8, NF), 0) < 4
    for ref, target in ((spec_ref, own_ref), (turn_ref, own_turn_ref)):
        for i in range(4):
            for k in range(S * W):
                first = jnp.broadcast_to(ref[8 * k + i : 8 * k + i + 1], (8, NF))
                second = jnp.broadcast_to(ref[8 * k + 4 + i : 8 * k + 5 + i], (8, NF))
                target[i, 8 * k : 8 * k + 8] = jnp.where(upper, first, second)
    lag_copy.wait()

    def pass_on(plane):
        for chip in range(2):
            src = 4 * plane + 2 * chip + core

            @pl.when(src != me)
            def _():
                copy_block(src, partner, pass_sem.at[src]).wait_recv()
                copy_block(src, partner, pass_sem.at[src]).start()

    quads = COLS // 4
    for chunk in range(n // COLS):

        def local_of(q):
            return lax.rem(me // 4 + quads - q, quads)

        pass_on(chunk * quads + local_of(0))

        def quad(q, carry):
            local = local_of(q)

            @pl.when(q < quads - 1)
            def _():
                pass_on(chunk * quads + local_of(q + 1))

            base = chunk * COLS + 4 * local
            for chip in range(2):
                src = base + 2 * chip + 1 - core
                copy_block(src, partner, pass_sem.at[src]).wait_recv()
            for i in range(4):
                for half, ref in enumerate((own_ref, own_turn_ref)):
                    sums = []
                    for d in range(4):
                        theirs = all_ref[base + d].astype(jnp.float32)
                        acc = ref[i, 0:8] * theirs[0:8]
                        for k in range(1, S * W):
                            acc = acc + ref[i, 8 * k : 8 * k + 8] * theirs[8 * k : 8 * k + 8]
                        sums.append(acc)
                    both = []
                    for d in (0, 2):
                        a, b = sums[d], sums[d + 1]
                        both.append(
                            jnp.where(upper, a, b) + pltpu.roll(jnp.where(upper, b, a), 4, 0)
                        )
                    high, low = split(jnp.concatenate(both, 0))
                    at = pl.ds(pl.multiple_of(4 * COLS * i + 16 * local, 16), 16)
                    cross_hi_ref[at, NF * half : NF * (half + 1)] = high
                    cross_lo_ref[at, NF * half : NF * (half + 1)] = low
            return carry

        lax.fori_loop(0, quads, quad, 0)
        lag = lag_ref[...]
        summed = product_nt(cross_hi_ref[...], lag)
        summed = (
            summed[:, :LAG_ROWS]
            + summed[:, LAG_ROWS:]
            + product_nt(cross_lo_ref[...], lag[:LAG_ROWS])
        )
        scale = masks[chunk] / jnp.maximum(summed[:, LAGS : LAGS + 1], 1.0)
        result = (summed * scale).astype(jnp.bfloat16)
        for i in range(4):
            out_ref[i, 4 * COLS * chunk : 4 * COLS * (chunk + 1), :] = result[
                4 * COLS * i : 4 * COLS * (i + 1), :LAGS
            ]

    copy_block(me, partner, send_sem.at[0]).wait_send()

    def sent(k, carry):
        own_copy(k).wait_send()
        src = lax.rem(me + 2 * k, n)
        copy_block(src, partner, pass_sem.at[src]).wait_send()
        return carry

    lax.fori_loop(1, n // 2, sent, 0, unroll=True)

    @pl.when(me < n - 1)
    def _():
        to_right.wait_send()

    @pl.when(me > 0)
    def _():
        to_left.wait_send()


def on_device(raw, fir, spatial_taps, flags, keep):
    n = lax.axis_size("chan")
    vmem = pl.BlockSpec(memory_space=pltpu.VMEM)
    hbm = pl.BlockSpec(memory_space=pltpu.HBM)
    out = pl.pallas_call(
        functools.partial(kernel, n),
        out_shape=pltpu.VMEM((4, 4 * n, LAGS), jnp.bfloat16),
        in_specs=[hbm] * 7,
        out_specs=vmem,
        scratch_shapes=[
            pltpu.VMEM(raw.shape, jnp.float32),
            pltpu.VMEM((1, TAPS), jnp.float32),
            pltpu.SMEM((SPAN,), jnp.float32),
            pltpu.SMEM((S, 4), jnp.int32),
            pltpu.VMEM((1, 4 * n), jnp.int32),
            pltpu.VMEM((NT, 4 * NF), jnp.bfloat16),
            pltpu.VMEM((2 * LAG_ROWS, 2 * NF), jnp.bfloat16),
            pltpu.VMEM((32, 384), jnp.float32),
            pltpu.VMEM((W, 24, 2 * NF), jnp.float32),
            pltpu.VMEM((TD // 16, 128), jnp.float32),
            pltpu.VMEM((ROWS, 2 * NF), jnp.float32),
            pltpu.VMEM((ROWS, NF), jnp.float32),
            pltpu.VMEM((ROWS, NF), jnp.float32),
            pltpu.VMEM((4, ROWS, NF), jnp.float32),
            pltpu.VMEM((4, ROWS, NF), jnp.float32),
            pltpu.VMEM((n, ROWS, NF), jnp.bfloat16),
            pltpu.VMEM((16 * COLS, 2 * NF), jnp.bfloat16),
            pltpu.VMEM((16 * COLS, 2 * NF), jnp.bfloat16),
            pltpu.SemaphoreType.DMA((7,)),
            pltpu.SemaphoreType.DMA((2,)),
            pltpu.SemaphoreType.DMA((2,)),
            pltpu.SemaphoreType.DMA((n // 2,)),
            pltpu.SemaphoreType.DMA((n,)),
            pltpu.SemaphoreType.DMA((n,)),
        ],
        compiler_params=pltpu.CompilerParams(
            collective_id=0, has_side_effects=True, vmem_limit_bytes=48 * 2**20
        ),
    )(
        *[
            pltpu.with_memory_space_constraint(value, pltpu.HBM)
            for value in (
                raw,
                fir.reshape(1, TAPS),
                spatial_taps,
                flags.T,
                keep.reshape(1, 4 * n),
                jnp.asarray(dft_table()),
                jnp.asarray(lag_table()),
            )
        ]
    )
    return jnp.swapaxes(out, 1, 2)


def solution(mesh):
    placed = (P(("groups", "chan"), None, None), P(), P(), P(("groups", "chan"), None), P())
    return jax.shard_map(
        on_device,
        mesh=mesh,
        in_specs=placed,
        out_specs=P(("groups", "chan"), None, None),
        check_vma=False,
    )
```
